256 devices in a mesh: row: 64 (over z, y, core), col: 4 (over x).
Axes of the slice: x: 4, y: 4, z: 8, core: 2. Of those that a mesh axis runs over, the one named last changes fastest.
Arguments:
- right_sides: float32 [8, 3, 40960], P(None, None, ('row', 'col')), may hold values from -20 to 20
- cosine: float32 [40960], P(('row', 'col')), may hold values from -1 to 1
- azimuth: float32 [40960], P(('row', 'col')), may hold values from -3.140625 to 3.140625
- radius: float32 [40960], P(('row', 'col')), may hold values from 0.97 to 1.03
- panel_area: float32 [40960], P(('row', 'col')), may hold values from 0.5 to 2
Outputs:
- next_block: float32 [8, 3, 40960], P(None, None, ('row', 'col'))
- coefficients: float32 [24, 8], replicated
The draws below stay inside these ranges and needn't reach their ends.
All inputs are finite; a program needn't handle non-finite values.
Results may differ from the reference program's by a relative error of at most 0.0003.
Values sent between devices are 32-bit elements; how exact they have to be, the bound alone decides.
A program may use at most 192 MiB of HBM per device.

```python
import math
import jax
import jax.numpy as jnp
from jax import lax

RHS = 8
PANELS = 40960


def draw_right_sides(key, part):
    key = jax.random.fold_in(key, 7)
    ramp_up = 1.0 + 2.0 * jnp.arange(PANELS, dtype=jnp.float32) / PANELS
    values = jnp.clip(jax.random.normal(key, (RHS, 3, PANELS), jnp.float32), -6.0, 6.0)
    return values * ramp_up[None, None, :]


def block_levels(own_key, shape, cuts, smallest, top_value):
    def one(axis_at, parts):
        draws = jax.random.uniform(jax.random.fold_in(jax.random.fold_in(own_key, 6), axis_at), (parts,), jnp.float32, smallest / len(cuts), top_value / len(cuts))
        return jnp.repeat(jnp.exp(draws), shape[axis_at] // parts).reshape((-1,) + (1,) * (len(shape) - axis_at - 1))

    level = one(*cuts[0])
    for cut in cuts[1:]:
        level = level * one(*cut)
    return level


def setup_inputs(seed: int = 0) -> dict:
    key_of = jax.random.split(jax.random.key(seed), 6)
    right_sides = draw_right_sides(jax.random.fold_in(key_of[5], 71), 0)
    cosine = jnp.clip(jax.random.uniform(key_of[1], (PANELS,), jnp.float32, -1.0, 1.0) * block_levels(key_of[1], (PANELS,), ((0, 256),), -0.4, 0.0), -1.0, 1.0)
    azimuth = jnp.clip(jax.random.uniform(key_of[2], (PANELS,), jnp.float32, -3.140625, 3.140625), -3.140625, 3.140625)
    radius = jnp.clip(0.97 + 0.059999943 * jax.random.uniform(key_of[3], (PANELS,), jnp.float32) ** block_levels(key_of[3], (PANELS,), ((0, 256),), -0.2, 0.2), 0.97, 1.03)
    panel_area = jnp.clip(jnp.exp(math.log(2.0) - 1.3862944 * jax.random.uniform(key_of[4], (PANELS,), jnp.float32) ** block_levels(key_of[4], (PANELS,), ((0, 256),), -0.2, 0.2)), 0.5, 2.0)
    return {"right_sides": right_sides, "cosine": cosine, "azimuth": azimuth, "radius": radius, "panel_area": panel_area}


highest = lax.Precision.HIGHEST
stokes_factor = -0.75 / math.pi

def panel_frame(cosine, azimuth, radius, panel_area, spacing):
    sine_part = jnp.sqrt(jnp.maximum(1.0 - cosine * cosine, 0.0))
    unit_dir = jnp.stack([sine_part * jnp.cos(azimuth), sine_part * jnp.sin(azimuth), cosine])
    return (radius[None, :] * unit_dir, unit_dir, panel_area * spacing)

def features(src_pos, vectors):
    plain_part = jnp.transpose(vectors, (1, 2, 0))
    moved_part = src_pos[None, :, :, None] * plain_part[:, None, :, :]
    moved_part = jnp.transpose(moved_part, (0, 2, 1, 3)).reshape(3, src_pos.shape[1], 24)
    return jnp.concatenate([plain_part, moved_part], axis=2)

def interact(running, targets, src_pos, src_normal, src_weight, feats, spacing):
    separation = targets[:, :, None] - src_pos[:, None, :]
    distance2 = lax.optimization_barrier(jnp.sum(separation * separation, axis=0)) + spacing
    inverse = lax.rsqrt(distance2)
    inverse5 = inverse * inverse * inverse * inverse * inverse
    normal_part = lax.optimization_barrier(jnp.sum(separation * src_normal[:, None, :], axis=0))
    strength = stokes_factor * src_weight[None, :] * normal_part * inverse5
    leverage = strength[None] * separation
    return running + jnp.einsum('bij,bjm->im', leverage, feats, precision=highest)

def assemble(summed, targets):
    target_count = summed.shape[0]
    direct = jnp.transpose(summed[:, :8])
    shifted = jnp.transpose(summed[:, 8:].reshape(target_count, 3, 8), (2, 1, 0))
    return targets[None] * direct[:, None, :] - shifted

def gram_of(first_set, second_set):
    return jnp.einsum('kan,lan->kl', first_set, second_set, precision=highest)

def project_out(projection, basis):
    return jnp.einsum('kl,kan->lan', projection, basis, precision=highest)

def orthonormal(vectors_in, matrix):
    lower_factor = jnp.linalg.cholesky(matrix)
    new_rows = []
    for k in range(vectors_in.shape[0]):
        current = vectors_in[k]
        for m in range(k):
            current = current - lower_factor[k, m] * new_rows[m]
        new_rows.append(current / lower_factor[k, k])
    return (jnp.stack(new_rows), lower_factor)

def apply_operator(vectors, positions, normals, weights, spacing):
    feats = features(positions, vectors)
    block_rows = math.gcd(PANELS, 128)
    block_count = PANELS // block_rows
    target_blocks = jnp.transpose(positions.reshape(3, block_count, block_rows), (1, 0, 2))

    def row_block(targets):
        zeros = jnp.zeros((block_rows, 32), jnp.float32)
        return interact(zeros, targets, positions, normals, weights, feats, spacing)
    partials = lax.map(row_block, target_blocks).reshape(PANELS, 32)
    return 0.5 * vectors + assemble(partials, positions)

def reference(right_sides, cosine, azimuth, radius, panel_area):
    spacing = 4.0 * math.pi / PANELS
    positions, normals, weights = panel_frame(cosine, azimuth, radius, panel_area, spacing)
    basis, lower_start = orthonormal(right_sides, gram_of(right_sides, right_sides))
    image = apply_operator(basis, positions, normals, weights, spacing)
    projection = gram_of(basis, image)
    remainder = image - project_out(projection, basis)
    next_block, lower_next = orthonormal(remainder, gram_of(remainder, remainder))
    coefficients = jnp.concatenate([jnp.transpose(lower_start), projection, jnp.transpose(lower_next)], axis=0)
    return (next_block, coefficients)
```

```python
import functools
import math

import jax
import jax.numpy as jnp
from jax import lax
from jax.experimental import pallas as pl
from jax.experimental.pallas import tpu as pltpu
from jax.sharding import PartitionSpec as P

f32 = jnp.float32
bf16 = jnp.bfloat16
MESH = pl.DeviceIdType.MESH
GROUP = 16
WIDTH = 160
SOURCES = GROUP * WIDTH
TARGETS = GROUP * WIDTH
COLS = 256
DEPTH = 512
CHUNK = 32
FEATS = 80
TARGET_TILES = TARGETS // COLS
SOURCE_TILES = SOURCES // DEPTH


def exact_dot(left, right, dims):
    return lax.dot_general(
        left, right, (dims, ((), ())), precision=lax.Precision.HIGHEST, preferred_element_type=f32
    )


def split(value, pieces):
    parts = []
    for _ in range(pieces):
        part = value.astype(bf16).astype(f32)
        parts.append(part)
        value = value - part
    return parts


def eliminate(matrix):
    row = lax.broadcasted_iota(jnp.int32, matrix.shape, 0)
    for k in range(8):
        scale = 1.0 / jnp.sqrt(matrix[k : k + 1, k : k + 1])
        pivot = matrix[k : k + 1, :] * scale
        column = matrix[:, k : k + 1] * scale
        matrix = jnp.where(row == k, pivot, jnp.where(row > k, matrix - column * pivot, matrix))
    return matrix


def kernel(
    spacing,
    x_ref,
    next_ref,
    coef_ref,
    src_buf,
    tgt_buf,
    columns,
    feats,
    rows,
    tile_a,
    tile_b,
    sums,
    outbox,
    inbox,
    d_buf,
    e_buf,
    src_send,
    src_recv,
    tgt_send,
    tgt_recv,
    out_send,
    out_recv,
    d_send,
    d_recv,
    e_send,
    e_recv,
):
    me_row = lax.axis_index("row")
    me_col = lax.axis_index("col")
    core = lax.rem(me_row, 2)
    y = lax.rem(lax.div(me_row, 2), 4)
    z = lax.div(me_row, 8)
    me_a = z * 2 + core
    me_b = y * 4 + me_col

    def peer_a(slot):
        return (lax.div(slot, 2) * 8 + y * 2 + lax.rem(slot, 2), me_col)

    def peer_b(slot):
        return (z * 8 + lax.div(slot, 4) * 2 + core, lax.rem(slot, 4))

    barrier = pltpu.get_barrier_semaphore()

    def greet(k, carry):
        pl.semaphore_signal(
            barrier, inc=1, device_id=peer_a(lax.rem(me_a + k, GROUP)), device_id_type=MESH
        )
        pl.semaphore_signal(
            barrier, inc=1, device_id=peer_b(lax.rem(me_b + k, GROUP)), device_id_type=MESH
        )
        return carry

    lax.fori_loop(1, GROUP, greet, 0)

    def copy(src, dst, send, recv, mine, slot, peer):
        return pltpu.make_async_remote_copy(
            src_ref=src,
            dst_ref=dst,
            send_sem=send.at[slot],
            recv_sem=recv.at[mine],
            device_id=peer,
            device_id_type=MESH,
        )

    def start_all(src_of, dst, send, recv, mine, peer):
        def one(k, carry):
            slot = lax.rem(mine + k, GROUP)
            copy(src_of(slot), dst.at[mine], send, recv, mine, slot, peer(slot)).start()
            return carry

        lax.fori_loop(1, GROUP, one, 0)

    def wait_all(src_of, dst, send, recv, mine, peer):
        def one(k, carry):
            slot = lax.rem(mine + k, GROUP)
            copy(src_of(slot), dst.at[slot], send, recv, slot, slot, peer(slot)).wait_recv()
            copy(src_of(slot), dst.at[slot], send, recv, slot, slot, peer(slot)).wait_send()
            return carry

        lax.fori_loop(1, GROUP, one, 0)

    cosine = x_ref[24:25, :]
    azimuth = x_ref[25:26, :]
    radius = x_ref[26:27, :]
    area = x_ref[27:28, :]
    sine_part = jnp.sqrt(jnp.maximum(1.0 - cosine * cosine, 0.0))
    pos0 = radius * (sine_part * jnp.cos(azimuth))
    pos1 = radius * (sine_part * jnp.sin(azimuth))
    pos2 = radius * cosine
    weight = (-0.75 / math.pi) * (area * spacing) / (2.0 * radius)
    nothing = jnp.zeros((3, WIDTH), f32)
    geo = jnp.concatenate([pos0, pos1, pos2, radius * radius, weight, nothing], axis=0)
    parts = [x_ref[8 * m : 8 * m + 8, :] for m in range(3)] + [geo]
    own_rest = jnp.concatenate([part[:, 128:WIDTH] for part in parts], axis=1)
    for m in range(4):
        src_buf[me_a, 8 * m : 8 * m + 8, :] = parts[m][:, :128]
    src_buf[me_a, 32:40, :] = own_rest
    tgt_buf[me_b, 0:8, :] = geo[:, :128]
    tgt_buf[me_b, 8:16, :] = own_rest

    pl.semaphore_wait(barrier, 2 * (GROUP - 1))
    src_args = (lambda slot: src_buf.at[me_a], src_buf, src_send, src_recv, me_a, peer_a)
    tgt_args = (lambda slot: tgt_buf.at[me_b], tgt_buf, tgt_send, tgt_recv, me_b, peer_b)
    start_all(*src_args)
    start_all(*tgt_args)
    wait_all(*src_args)
    wait_all(*tgt_args)

    def put_sources(tile, place, group, parts):
        lanes = slice(128 * place, 128 * place + 128)
        geo = parts[3]
        scaled = [split(parts[c] * geo[4:5, :], 2) for c in range(3)]
        along = sum(geo[c : c + 1, :] * (scaled[c][0] + scaled[c][1]) for c in range(3))
        pieces = [scaled[c][p] for p in range(2) for c in range(3)] + split(along, 3)
        pieces.append(jnp.zeros((8, 128), f32))
        feats[tile, :, lanes] = jnp.concatenate(pieces, axis=0).astype(bf16)
        turned = jnp.transpose(geo)
        for a in range(4):
            columns[a, pl.ds(pl.multiple_of(128 * group, 128), 128), :] = jnp.broadcast_to(
                turned[:, a : a + 1], (128, 128)
            )

    def main_sources(tile, carry):
        for place in range(4):
            slot = tile * 4 + place
            parts = [src_buf[slot, 8 * m : 8 * m + 8, :] for m in range(4)]
            put_sources(tile, place, slot, parts)
        return carry

    lax.fori_loop(0, 4, main_sources, 0)
    for place in range(4):
        parts = [
            jnp.concatenate(
                [src_buf[4 * place + d, 32:40, 32 * m : 32 * m + 32] for d in range(4)], axis=1
            )
            for m in range(4)
        ]
        put_sources(4, place, 16 + place, parts)

    for tile in range(8):
        rows[tile] = jnp.concatenate([tgt_buf[2 * tile, 0:8, :], tgt_buf[2 * tile + 1, 0:8, :]], axis=1)
    for tile in range(2):
        rows[8 + tile] = jnp.concatenate(
            [tgt_buf[8 * tile + d, 8:16, 96:128] for d in range(8)], axis=1
        )

    def pair_parts(target_tile, source_tile, tile_ref):
        target = [rows[target_tile, a : a + 1, :] for a in range(3)]
        reach = rows[target_tile, 3:4, :] + spacing

        def one(c):
            at = pl.ds(pl.multiple_of(source_tile * DEPTH + c * CHUNK, CHUNK), CHUNK)

            def column(a):
                value = columns[a, at, :]
                return jnp.concatenate([value] * (COLS // 128), axis=1)

            r = [target[a] - column(a) for a in range(3)]
            dist = (r[0] * r[0] + spacing) + r[1] * r[1] + r[2] * r[2]
            inv = lax.rsqrt(dist)
            inv2 = inv * inv
            strength = (((reach - column(3)) - dist) * inv) * (inv2 * inv2)
            for a in range(3):
                value = strength * r[a]
                high = value.astype(bf16)
                tile_ref[a, 0, c * CHUNK : (c + 1) * CHUNK, :] = high
                tile_ref[a, 1, c * CHUNK : (c + 1) * CHUNK, :] = (value - high.astype(f32)).astype(bf16)

        return [functools.partial(one, c) for c in range(DEPTH // CHUNK)]

    def sum_parts(target_tile, source_tile, tile_ref):
        def one(a):
            left = feats[source_tile]
            sums[target_tile, a] += jnp.dot(
                left, tile_ref[a, 0], preferred_element_type=f32
            ) + jnp.dot(left, tile_ref[a, 1], preferred_element_type=f32)

        return [functools.partial(one, a) for a in range(3)]

    def mixed(firsts, seconds):
        order = [((i + 0.5) / len(firsts), 0, f) for i, f in enumerate(firsts)]
        order += [((i + 0.3) / len(seconds), 1, f) for i, f in enumerate(seconds)]
        for _, _, f in sorted(order, key=lambda item: item[:2]):
            f()

    steps = TARGET_TILES * SOURCE_TILES
    for tile in range(TARGET_TILES):
        sums[tile] = jnp.zeros((3, FEATS, COLS), f32)
    for f in pair_parts(0, 0, tile_a):
        f()

    def place_of(step):
        return lax.div(step, SOURCE_TILES), lax.rem(step, SOURCE_TILES)

    def advance(turn, carry):
        here = place_of(2 * turn)
        after = place_of(2 * turn + 1)
        later = place_of(jnp.minimum(2 * turn + 2, steps - 1))

        @pl.when(turn < steps)
        def _():
            mixed(pair_parts(*after, tile_b), sum_parts(*here, tile_a))

        @pl.when(turn < steps + 1)
        def _():
            mixed(pair_parts(*later, tile_a), sum_parts(*after, tile_b))

        return carry

    lax.fori_loop(0, steps // 2, advance, 0)

    def images(tile):
        found = []
        for a in range(3):
            total = sums[tile, a]
            image = -(total[48:56] + total[56:64] + total[64:72])
            for c in range(3):
                image = image + rows[tile, c : c + 1, :] * (
                    total[8 * c : 8 * c + 8] + total[24 + 8 * c : 32 + 8 * c]
                )
            found.append(image)
        return found

    def main_images(tile, carry):
        found = images(tile)
        for half in range(2):
            for a in range(3):
                outbox[2 * tile + half, 8 * a : 8 * a + 8, :] = found[a][:, 128 * half : 128 * half + 128]
        return carry

    lax.fori_loop(0, 8, main_images, 0)
    for tile in range(2):
        found = images(8 + tile)
        for d in range(8):
            lanes = slice(32 * d, 32 * d + 32)
            outbox[8 * tile + d, 24:32, :] = jnp.concatenate(
                [found[a][:, lanes] for a in range(3)] + [jnp.zeros((8, 32), f32)], axis=1
            )

    out_args = (lambda slot: outbox.at[slot], inbox, out_send, out_recv, me_b, peer_b)
    start_all(*out_args)
    inbox[me_b] = outbox[me_b]
    wait_all(*out_args)
    image = inbox[0]
    for slot in range(1, GROUP):
        image = image + inbox[slot]

    lane = lax.broadcasted_iota(jnp.int32, (8, 128), 1)
    own = [src_buf[me_a, 8 * m : 8 * m + 8, :] for m in range(3)]
    own.append(jnp.where(lane < 96, src_buf[me_a, 32:40, :], 0.0))
    right = jnp.concatenate(own, axis=1)
    pushed = jnp.concatenate([image[8 * m : 8 * m + 8, :] for m in range(4)], axis=1)
    both = jnp.concatenate([right, pushed], axis=0)
    gram = exact_dot(both, both, ((1,), (1,)))
    d_buf[me_b] = jnp.concatenate([gram, jnp.zeros((16, 112), f32)], axis=1)
    d_args = (lambda slot: d_buf.at[me_b], d_buf, d_send, d_recv, me_b, peer_b)
    start_all(*d_args)
    wait_all(*d_args)
    gram = d_buf[0]
    for slot in range(1, GROUP):
        gram = gram + d_buf[slot]
    e_buf[me_a] = gram
    e_args = (lambda slot: e_buf.at[me_a], e_buf, e_send, e_recv, me_a, peer_a)
    start_all(*e_args)
    wait_all(*e_args)
    gram = e_buf[0]
    for slot in range(1, GROUP):
        gram = gram + e_buf[slot]

    row8 = lax.broadcasted_iota(jnp.int32, (8, 8), 0)
    lane8 = lax.broadcasted_iota(jnp.int32, (8, 8), 1)
    unit = jnp.where(row8 == lane8, 1.0, 0.0)
    first = eliminate(jnp.concatenate([gram[0:8, 0:8], unit, gram[0:8, 8:16]], axis=1))
    inverse = first[:, 8:16]
    moved = exact_dot(first[:, 16:24], inverse, ((1,), (1,)))
    image_gram = exact_dot(
        exact_dot(inverse, gram[8:16, 8:16], ((1,), (0,))), inverse, ((1,), (1,))
    )
    remainder_gram = image_gram - exact_dot(moved, moved, ((0,), (0,)))
    back = exact_dot(moved, inverse, ((0,), (0,)))
    second = eliminate(jnp.concatenate([remainder_gram, inverse, -back], axis=1))
    stacked = jnp.concatenate([pushed, right], axis=0)
    result = exact_dot(second[:, 8:24], stacked, ((1,), (0,)))
    for c in range(3):
        next_ref[c, :, 0:128] = result[:, 128 * c : 128 * c + 128]
        next_ref[c, :, 128:WIDTH] = result[:, 384 + 32 * c : 416 + 32 * c]
    coef_ref[0:8, :] = jnp.where(lane8 >= row8, first[:, 0:8], 0.0)
    coef_ref[8:16, :] = moved + 0.5 * unit
    coef_ref[16:24, :] = jnp.where(lane8 >= row8, second[:, 0:8], 0.0)


def shards(right_sides, cosine, azimuth, radius, panel_area):
    width = cosine.shape[0]
    total = width * lax.axis_size("row") * lax.axis_size("col")
    spacing = 4.0 * math.pi / total
    packed = jnp.concatenate(
        [
            jnp.transpose(right_sides, (1, 0, 2)).reshape(24, width),
            jnp.stack([cosine, azimuth, radius, panel_area]),
            jnp.zeros((4, width), f32),
        ],
        axis=0,
    )
    dma = pltpu.SemaphoreType.DMA((GROUP,))
    next_block, coefficients = pl.pallas_call(
        functools.partial(kernel, spacing),
        out_shape=(
            jax.ShapeDtypeStruct((3, 8, width), f32),
            jax.ShapeDtypeStruct((24, 8), f32),
        ),
        in_specs=[pl.BlockSpec(memory_space=pltpu.VMEM)],
        out_specs=(pl.BlockSpec(memory_space=pltpu.VMEM), pl.BlockSpec(memory_space=pltpu.VMEM)),
        scratch_shapes=[
            pltpu.VMEM((GROUP, 40, 128), f32),
            pltpu.VMEM((GROUP, 16, 128), f32),
            pltpu.VMEM((4, SOURCES, 128), f32),
            pltpu.VMEM((SOURCE_TILES, FEATS, DEPTH), bf16),
            pltpu.VMEM((TARGET_TILES, 8, COLS), f32),
            pltpu.VMEM((3, 2, DEPTH, COLS), bf16),
            pltpu.VMEM((3, 2, DEPTH, COLS), bf16),
            pltpu.VMEM((TARGET_TILES, 3, FEATS, COLS), f32),
            pltpu.VMEM((GROUP, 32, 128), f32),
            pltpu.VMEM((GROUP, 32, 128), f32),
            pltpu.VMEM((GROUP, 16, 128), f32),
            pltpu.VMEM((GROUP, 16, 128), f32),
        ]
        + [dma] * 10,
        compiler_params=pltpu.CompilerParams(
            collective_id=0, has_side_effects=True, vmem_limit_bytes=40 << 20
        ),
        name="arnoldi_step",
    )(packed)
    return jnp.transpose(next_block, (1, 0, 2)), coefficients


def solution(mesh):
    placed = (
        P(None, None, ("row", "col")),
        P(("row", "col")),
        P(("row", "col")),
        P(("row", "col")),
        P(("row", "col")),
    )
    return jax.shard_map(
        shards,
        mesh=mesh,
        in_specs=placed,
        out_specs=(P(None, None, ("row", "col")), P()),
        check_vma=False,
    )
```

```python
import functools
import math

import jax
import jax.numpy as jnp
from jax import lax
from jax.experimental import pallas as pl
from jax.experimental.pallas import tpu as pltpu
from jax.sharding import PartitionSpec as P

f32 = jnp.float32
bf16 = jnp.bfloat16
MESH = pl.DeviceIdType.MESH
LINE = 4
GROUP = 16
WIDTH = 160
SOURCES = GROUP * WIDTH
TARGETS = GROUP * WIDTH
COLS = 256
DEPTH = 512
CHUNK = 32
FEATS = 80
TARGET_TILES = TARGETS // COLS
SOURCE_TILES = SOURCES // DEPTH


def exact_dot(left, right, dims):
    return lax.dot_general(
        left, right, (dims, ((), ())), precision=lax.Precision.HIGHEST, preferred_element_type=f32
    )


def split(value, pieces):
    parts = []
    for _ in range(pieces):
        part = value.astype(bf16).astype(f32)
        parts.append(part)
        value = value - part
    return parts


def eliminate(matrix):
    row = lax.broadcasted_iota(jnp.int32, matrix.shape, 0)
    for k in range(8):
        scale = 1.0 / jnp.sqrt(matrix[k : k + 1, k : k + 1])
        pivot = matrix[k : k + 1, :] * scale
        column = matrix[:, k : k + 1] * scale
        matrix = jnp.where(row == k, pivot, jnp.where(row > k, matrix - column * pivot, matrix))
    return matrix


def kernel(
    spacing,
    x_ref,
    next_ref,
    coef_ref,
    src_buf,
    tgt_buf,
    columns,
    feats,
    rows,
    tile_a,
    tile_b,
    sums,
    outbox,
    inbox_y,
    out_line,
    inbox_x,
    gx_buf,
    gy_buf,
    gz_buf,
    gc_buf,
    sz_send,
    sz_recv,
    sc_send,
    sc_recv,
    tx_send,
    tx_recv,
    ty_send,
    ty_recv,
    oy_send,
    oy_recv,
    ox_send,
    ox_recv,
    gx_send,
    gx_recv,
    gy_send,
    gy_recv,
    gz_send,
    gz_recv,
    gc_send,
    gc_recv,
):
    me_row = lax.axis_index("row")
    me_x = lax.axis_index("col")
    core = lax.rem(me_row, 2)
    me_y = lax.rem(lax.div(me_row, 2), LINE)
    me_z = lax.div(me_row, 8)
    me_a = core * 8 + me_z
    me_b = me_y * LINE + me_x

    def peer_x(slot):
        return (me_row, slot)

    def peer_y(slot):
        return (me_z * 8 + slot * 2 + core, me_x)

    def peer_z(slot):
        return (slot * 8 + me_y * 2 + core, me_x)

    def peer_core(slot):
        return (me_z * 8 + me_y * 2 + slot, me_x)

    lines = ((peer_x, me_x, LINE), (peer_y, me_y, LINE), (peer_z, me_z, 8), (peer_core, core, 2))
    barrier = pltpu.get_barrier_semaphore()
    for peer, mine, count in lines:

        def greet(k, carry, peer=peer, mine=mine, count=count):
            pl.semaphore_signal(
                barrier, inc=1, device_id=peer(lax.rem(mine + k, count)), device_id_type=MESH
            )
            return carry

        lax.fori_loop(1, count, greet, 0)

    class Exchange:
        def __init__(self, line, src_of, dst_of, send, recv):
            self.peer, self.mine, self.count = lines[line]
            self.src_of, self.dst_of, self.send, self.recv = src_of, dst_of, send, recv

        def copy(self, slot, landing):
            return pltpu.make_async_remote_copy(
                src_ref=self.src_of(slot),
                dst_ref=self.dst_of(landing),
                send_sem=self.send.at[slot],
                recv_sem=self.recv.at[landing],
                device_id=self.peer(slot),
                device_id_type=MESH,
            )

        def each(self, act):
            def one(k, carry):
                act(lax.rem(self.mine + k, self.count))
                return carry

            lax.fori_loop(1, self.count, one, 0)

        def start(self):
            self.each(lambda slot: self.copy(slot, self.mine).start())

        def wait(self):
            self.each(lambda slot: self.copy(slot, slot).wait_recv())

        def finish(self):
            self.each(lambda slot: self.copy(slot, slot).wait_send())

    def group(buf, slot, count):
        return buf.at[pl.ds(slot * count, count)]

    src_z = Exchange(
        2, lambda s: src_buf.at[me_a], lambda s: src_buf.at[core * 8 + s], sz_send, sz_recv
    )
    src_core = Exchange(
        3, lambda s: group(src_buf, core, 8), lambda s: group(src_buf, s, 8), sc_send, sc_recv
    )
    tgt_x = Exchange(
        0, lambda s: tgt_buf.at[me_b], lambda s: tgt_buf.at[me_y * LINE + s], tx_send, tx_recv
    )
    tgt_y = Exchange(
        1,
        lambda s: group(tgt_buf, me_y, LINE),
        lambda s: group(tgt_buf, s, LINE),
        ty_send,
        ty_recv,
    )
    out_y = Exchange(
        1, lambda s: group(outbox, s, LINE), lambda s: group(inbox_y, s, LINE), oy_send, oy_recv
    )
    out_x = Exchange(0, lambda s: out_line.at[s], lambda s: inbox_x.at[s], ox_send, ox_recv)
    totals = [
        Exchange(line, lambda s, b=b, m=m: b.at[m], lambda s, b=b: b.at[s], send, recv)
        for line, (b, m, send, recv) in enumerate(
            (
                (gx_buf, me_x, gx_send, gx_recv),
                (gy_buf, me_y, gy_send, gy_recv),
                (gz_buf, me_z, gz_send, gz_recv),
                (gc_buf, core, gc_send, gc_recv),
            )
        )
    ]

    cosine = x_ref[24:25, :]
    azimuth = x_ref[25:26, :]
    radius = x_ref[26:27, :]
    area = x_ref[27:28, :]
    sine_part = jnp.sqrt(jnp.maximum(1.0 - cosine * cosine, 0.0))
    pos0 = radius * (sine_part * jnp.cos(azimuth))
    pos1 = radius * (sine_part * jnp.sin(azimuth))
    pos2 = radius * cosine
    weight = (-0.75 / math.pi) * (area * spacing) / (2.0 * radius)
    nothing = jnp.zeros((3, WIDTH), f32)
    geo = jnp.concatenate([pos0, pos1, pos2, radius * radius, weight, nothing], axis=0)
    parts = [x_ref[8 * m : 8 * m + 8, :] for m in range(3)] + [geo]
    own_rest = jnp.concatenate([part[:, 128:WIDTH] for part in parts], axis=1)
    for m in range(4):
        src_buf[me_a, 8 * m : 8 * m + 8, :] = parts[m][:, :128]
    src_buf[me_a, 32:40, :] = own_rest
    tgt_buf[me_b, 0:8, :] = geo[:, :128]
    tgt_buf[me_b, 8:16, :] = own_rest

    pl.semaphore_wait(barrier, sum(count - 1 for _, _, count in lines))
    tgt_x.start()
    src_z.start()
    tgt_x.wait()
    tgt_y.start()

    def put_sources(tile, place, group, parts):
        lanes = slice(128 * place, 128 * place + 128)
        geo = parts[3]
        scaled = [split(parts[c] * geo[4:5, :], 2) for c in range(3)]
        along = sum(geo[c : c + 1, :] * (scaled[c][0] + scaled[c][1]) for c in range(3))
        pieces = [scaled[c][p] for p in range(2) for c in range(3)] + split(along, 3)
        pieces.append(jnp.zeros((8, 128), f32))
        feats[tile, :, lanes] = jnp.concatenate(pieces, axis=0).astype(bf16)
        turned = jnp.transpose(geo)
        for a in range(4):
            columns[a, pl.ds(pl.multiple_of(128 * group, 128), 128), :] = jnp.broadcast_to(
                turned[:, a : a + 1], (128, 128)
            )

    def main_sources(tile, first_slot):
        for place in range(4):
            slot = first_slot + place
            parts = [src_buf[slot, 8 * m : 8 * m + 8, :] for m in range(4)]
            put_sources(tile, place, tile * 4 + place, parts)

    def rest_sources():
        for place in range(4):
            parts = [
                jnp.concatenate(
                    [src_buf[4 * place + d, 32:40, 32 * m : 32 * m + 32] for d in range(4)], axis=1
                )
                for m in range(4)
            ]
            put_sources(4, place, 16 + place, parts)

    for tile in range(TARGET_TILES):
        sums[tile] = jnp.zeros((3, FEATS, COLS), f32)
    src_z.wait()
    src_core.start()

    def near(tile, carry):
        main_sources(tile, core * 8 + tile * 4)
        return carry

    lax.fori_loop(0, 2, near, 0)
    tgt_y.wait()
    for tile in range(8):
        rows[tile] = jnp.concatenate([tgt_buf[2 * tile, 0:8, :], tgt_buf[2 * tile + 1, 0:8, :]], axis=1)
    for tile in range(2):
        rows[8 + tile] = jnp.concatenate(
            [tgt_buf[8 * tile + d, 8:16, 96:128] for d in range(8)], axis=1
        )

    def pair_parts(target_tile, source_tile, tile_ref):
        target = [rows[target_tile, a : a + 1, :] for a in range(3)]
        reach = rows[target_tile, 3:4, :] + spacing

        def one(c):
            at = pl.ds(pl.multiple_of(source_tile * DEPTH + c * CHUNK, CHUNK), CHUNK)

            def column(a):
                value = columns[a, at, :]
                return jnp.concatenate([value] * (COLS // 128), axis=1)

            r = [target[a] - column(a) for a in range(3)]
            dist = (r[0] * r[0] + spacing) + r[1] * r[1] + r[2] * r[2]
            inv = lax.rsqrt(dist)
            inv2 = inv * inv
            strength = (((reach - column(3)) - dist) * inv) * (inv2 * inv2)
            for a in range(3):
                value = strength * r[a]
                high = value.astype(bf16)
                tile_ref[a, 0, c * CHUNK : (c + 1) * CHUNK, :] = high
                tile_ref[a, 1, c * CHUNK : (c + 1) * CHUNK, :] = (value - high.astype(f32)).astype(bf16)

        return [functools.partial(one, c) for c in range(DEPTH // CHUNK)]

    def sum_parts(target_tile, source_tile, tile_ref):
        def one(a):
            left = feats[source_tile]
            sums[target_tile, a] += jnp.dot(
                left, tile_ref[a, 0], preferred_element_type=f32
            ) + jnp.dot(left, tile_ref[a, 1], preferred_element_type=f32)

        return [functools.partial(one, a) for a in range(3)]

    def mixed(firsts, seconds):
        order = [((i + 0.5) / len(firsts), 0, f) for i, f in enumerate(firsts)]
        order += [((i + 0.3) / len(seconds), 1, f) for i, f in enumerate(seconds)]
        for _, _, f in sorted(order, key=lambda item: item[:2]):
            f()

    def images(tile):
        found = []
        for a in range(3):
            total = sums[tile, a]
            image = -(total[48:56] + total[56:64] + total[64:72])
            for c in range(3):
                image = image + rows[tile, c : c + 1, :] * (
                    total[8 * c : 8 * c + 8] + total[24 + 8 * c : 32 + 8 * c]
                )
            found.append(image)
        return found

    pairs = TARGET_TILES // 2
    turns = pairs * SOURCE_TILES

    def place_of(turn):
        source = lax.div(turn, pairs)
        pair = lax.rem(turn, pairs)
        ordered = jnp.where(pair == 0, pairs - 1, lax.rem(me_y + pair, LINE))
        return source, 2 * jnp.where(source == SOURCE_TILES - 1, ordered, pair)

    first_source, first_target = place_of(0)
    for f in pair_parts(first_target, first_source, tile_a):
        f()

    def advance(turn, carry):
        source, target = place_of(turn)
        later_source, later_target = place_of(jnp.minimum(turn + 1, turns - 1))

        @pl.when(turn == 2 * pairs - 1)
        def _():
            src_core.wait()

            def far(tile, carry):
                main_sources(tile, (1 - core) * 8 + (tile - 2) * 4)
                return carry

            lax.fori_loop(2, 4, far, 0)
            rest_sources()

        @pl.when(turn < turns)
        def _():
            mixed(pair_parts(target + 1, source, tile_b), sum_parts(target, source, tile_a))

        @pl.when(turn < turns + 1)
        def _():
            mixed(
                pair_parts(later_target, later_source, tile_a),
                sum_parts(target + 1, source, tile_b),
            )

        last = source == SOURCE_TILES - 1

        @pl.when(jnp.logical_and(last, target == 8))
        def _():
            for tile in range(2):
                found = images(8 + tile)
                for d in range(8):
                    lanes = slice(32 * d, 32 * d + 32)
                    outbox[8 * tile + d, 24:32, :] = jnp.concatenate(
                        [found[a][:, lanes] for a in range(3)] + [jnp.zeros((8, 32), f32)], axis=1
                    )

        @pl.when(jnp.logical_and(last, target < 8))
        def _():
            for tile in range(2):
                found = images(target + tile)
                for half in range(2):
                    for a in range(3):
                        outbox[2 * (target + tile) + half, 8 * a : 8 * a + 8, :] = found[a][
                            :, 128 * half : 128 * half + 128
                        ]

        @pl.when(jnp.logical_and(last, jnp.logical_and(target < 8, target != 2 * me_y)))
        def _():
            slot = lax.div(target, 2)
            out_y.copy(slot, me_y).start()

        return carry

    lax.fori_loop(0, turns, advance, 0)

    inbox_y[pl.ds(me_y * LINE, LINE)] = outbox[pl.ds(me_y * LINE, LINE)]
    out_y.wait()
    for slot in range(LINE):
        out_line[slot] = (inbox_y[slot] + inbox_y[LINE + slot]) + (
            inbox_y[2 * LINE + slot] + inbox_y[3 * LINE + slot]
        )
    out_x.start()
    inbox_x[me_x] = out_line[me_x]
    out_x.wait()
    image = (inbox_x[0] + inbox_x[1]) + (inbox_x[2] + inbox_x[3])

    lane = lax.broadcasted_iota(jnp.int32, (8, 128), 1)
    own = [src_buf[me_a, 8 * m : 8 * m + 8, :] for m in range(3)]
    own.append(jnp.where(lane < 96, src_buf[me_a, 32:40, :], 0.0))
    right = jnp.concatenate(own, axis=1)
    pushed = jnp.concatenate([image[8 * m : 8 * m + 8, :] for m in range(4)], axis=1)
    both = jnp.concatenate([right, pushed], axis=0)
    gram = exact_dot(both, both, ((1,), (1,)))
    gram = jnp.concatenate([gram[0:8], gram[8:16], jnp.zeros((8, 96), f32)], axis=1)
    for total, buf in zip(totals, (gx_buf, gy_buf, gz_buf, gc_buf)):
        buf[total.mine] = gram
        total.start()
        total.wait()
        gram = buf[0]
        for slot in range(1, total.count):
            gram = gram + buf[slot]

    row8 = lax.broadcasted_iota(jnp.int32, (8, 8), 0)
    lane8 = lax.broadcasted_iota(jnp.int32, (8, 8), 1)
    unit = jnp.where(row8 == lane8, 1.0, 0.0)
    first = eliminate(jnp.concatenate([gram[:, 0:8], unit, gram[:, 8:16]], axis=1))
    inverse = first[:, 8:16]
    moved = exact_dot(first[:, 16:24], inverse, ((1,), (1,)))
    image_gram = exact_dot(
        exact_dot(inverse, gram[:, 24:32], ((1,), (0,))), inverse, ((1,), (1,))
    )
    remainder_gram = image_gram - exact_dot(moved, moved, ((0,), (0,)))
    back = exact_dot(moved, inverse, ((0,), (0,)))
    second = eliminate(jnp.concatenate([remainder_gram, inverse, -back], axis=1))
    stacked = jnp.concatenate([pushed, right], axis=0)
    result = exact_dot(second[:, 8:24], stacked, ((1,), (0,)))
    for c in range(3):
        next_ref[c, :, 0:128] = result[:, 128 * c : 128 * c + 128]
        next_ref[c, :, 128:WIDTH] = result[:, 384 + 32 * c : 416 + 32 * c]
    coef_ref[0:8, :] = jnp.where(lane8 >= row8, first[:, 0:8], 0.0)
    coef_ref[8:16, :] = moved + 0.5 * unit
    coef_ref[16:24, :] = jnp.where(lane8 >= row8, second[:, 0:8], 0.0)

    for exchange in [tgt_x, src_z, tgt_y, src_core, out_y, out_x] + totals:
        exchange.finish()


def shards(right_sides, cosine, azimuth, radius, panel_area):
    width = cosine.shape[0]
    total = width * lax.axis_size("row") * lax.axis_size("col")
    spacing = 4.0 * math.pi / total
    packed = jnp.concatenate(
        [
            jnp.transpose(right_sides, (1, 0, 2)).reshape(24, width),
            jnp.stack([cosine, azimuth, radius, panel_area]),
            jnp.zeros((4, width), f32),
        ],
        axis=0,
    )
    next_block, coefficients = pl.pallas_call(
        functools.partial(kernel, spacing),
        out_shape=(
            jax.ShapeDtypeStruct((3, 8, width), f32),
            jax.ShapeDtypeStruct((24, 8), f32),
        ),
        in_specs=[pl.BlockSpec(memory_space=pltpu.VMEM)],
        out_specs=(pl.BlockSpec(memory_space=pltpu.VMEM), pl.BlockSpec(memory_space=pltpu.VMEM)),
        scratch_shapes=[
            pltpu.VMEM((GROUP, 40, 128), f32),
            pltpu.VMEM((GROUP, 16, 128), f32),
            pltpu.VMEM((4, SOURCES, 128), f32),
            pltpu.VMEM((SOURCE_TILES, FEATS, DEPTH), bf16),
            pltpu.VMEM((TARGET_TILES, 8, COLS), f32),
            pltpu.VMEM((3, 2, DEPTH, COLS), bf16),
            pltpu.VMEM((3, 2, DEPTH, COLS), bf16),
            pltpu.VMEM((TARGET_TILES, 3, FEATS, COLS), f32),
            pltpu.VMEM((GROUP, 32, 128), f32),
            pltpu.VMEM((GROUP, 32, 128), f32),
            pltpu.VMEM((LINE, 32, 128), f32),
            pltpu.VMEM((LINE, 32, 128), f32),
            pltpu.VMEM((LINE, 8, 128), f32),
            pltpu.VMEM((LINE, 8, 128), f32),
            pltpu.VMEM((8, 8, 128), f32),
            pltpu.VMEM((2, 8, 128), f32),
        ]
        + [pltpu.SemaphoreType.DMA((8,))] * 20,
        compiler_params=pltpu.CompilerParams(
            collective_id=0, has_side_effects=True, vmem_limit_bytes=40 << 20
        ),
        name="arnoldi_step",
    )(packed)
    return jnp.transpose(next_block, (1, 0, 2)), coefficients


def solution(mesh):
    placed = (
        P(None, None, ("row", "col")),
        P(("row", "col")),
        P(("row", "col")),
        P(("row", "col")),
        P(("row", "col")),
    )
    return jax.shard_map(
        shards,
        mesh=mesh,
        in_specs=placed,
        out_specs=(P(None, None, ("row", "col")), P()),
        check_vma=False,
    )
```

```python
import functools
import math

import jax
import jax.numpy as jnp
from jax import lax
from jax.experimental import pallas as pl
from jax.experimental.pallas import tpu as pltpu
from jax.sharding import PartitionSpec as P

f32 = jnp.float32
bf16 = jnp.bfloat16
MESH = pl.DeviceIdType.MESH
NEAREST = (1, 7, 2, 6, 3, 5, 4)
LINE = 4
GROUP = 16
WIDTH = 160
SOURCES = GROUP * WIDTH
TARGETS = GROUP * WIDTH
COLS = 256
DEPTH = 512
CHUNK = 32
FEATS = 80
TARGET_TILES = TARGETS // COLS
SOURCE_TILES = SOURCES // DEPTH


def exact_dot(left, right, dims):
    return lax.dot_general(
        left, right, (dims, ((), ())), precision=lax.Precision.HIGHEST, preferred_element_type=f32
    )


def split(value, pieces):
    parts = []
    for _ in range(pieces):
        part = value.astype(bf16).astype(f32)
        parts.append(part)
        value = value - part
    return parts


def eliminate(matrix):
    row = lax.broadcasted_iota(jnp.int32, matrix.shape, 0)
    for k in range(8):
        scale = 1.0 / jnp.sqrt(matrix[k : k + 1, k : k + 1])
        pivot = matrix[k : k + 1, :] * scale
        column = matrix[:, k : k + 1] * scale
        matrix = jnp.where(row == k, pivot, jnp.where(row > k, matrix - column * pivot, matrix))
    return matrix


def kernel(
    spacing,
    right_ref,
    cosine_ref,
    azimuth_ref,
    radius_ref,
    area_ref,
    next_ref,
    coef_ref,
    src_buf,
    tgt_buf,
    columns,
    feats,
    rows,
    tile_a,
    tile_b,
    sums,
    outbox,
    inbox,
    gb_buf,
    ga_buf,
    sz_send,
    sz_recv,
    sc_send,
    sc_recv,
    tgt_send,
    tgt_recv,
    out_send,
    out_recv,
    gb_send,
    gb_recv,
    ga_send,
    ga_recv,
):
    me_row = lax.axis_index("row")
    me_x = lax.axis_index("col")
    core = lax.rem(me_row, 2)
    me_y = lax.rem(lax.div(me_row, 2), LINE)
    me_z = lax.div(me_row, 8)
    me_a = core * 8 + me_z
    me_b = me_y * LINE + me_x

    def peer_z(slot):
        return (slot * 8 + me_y * 2 + core, me_x)

    def peer_core(slot):
        return (me_z * 8 + me_y * 2 + slot, me_x)

    def peer_a(slot):
        return (lax.rem(slot, 8) * 8 + me_y * 2 + lax.div(slot, 8), me_x)

    def peer_b(slot):
        return (me_z * 8 + lax.div(slot, LINE) * 2 + core, lax.rem(slot, LINE))

    lines = ((peer_z, me_z, 8), (peer_core, core, 2), (peer_b, me_b, GROUP), (peer_a, me_a, GROUP))
    barrier = pltpu.get_barrier_semaphore()
    for peer, mine, count in lines[:3]:

        def greet(k, carry, peer=peer, mine=mine, count=count):
            pl.semaphore_signal(
                barrier, inc=1, device_id=peer(lax.rem(mine + k, count)), device_id_type=MESH
            )
            return carry

        lax.fori_loop(1, count, greet, 0)

    class Exchange:
        def __init__(self, line, src_of, dst_of, send, recv):
            self.peer, self.mine, self.count = lines[line]
            self.src_of, self.dst_of, self.send, self.recv = src_of, dst_of, send, recv

        def copy(self, slot, landing):
            return pltpu.make_async_remote_copy(
                src_ref=self.src_of(slot),
                dst_ref=self.dst_of(landing),
                send_sem=self.send.at[slot],
                recv_sem=self.recv.at[landing],
                device_id=self.peer(slot),
                device_id_type=MESH,
            )

        def each(self, act):
            def one(k, carry):
                act(lax.rem(self.mine + k, self.count))
                return carry

            lax.fori_loop(1, self.count, one, 0)

        def start(self):
            self.each(lambda slot: self.copy(slot, self.mine).start())

        def wait(self):
            self.each(lambda slot: self.copy(slot, slot).wait_recv())

        def finish(self):
            self.each(lambda slot: self.copy(slot, slot).wait_send())

    def group(buf, slot, count):
        return buf.at[pl.ds(slot * count, count)]

    src_z = Exchange(
        0, lambda s: src_buf.at[me_a], lambda s: src_buf.at[core * 8 + s], sz_send, sz_recv
    )
    src_core = Exchange(
        1, lambda s: group(src_buf, core, 8), lambda s: group(src_buf, s, 8), sc_send, sc_recv
    )
    tgt = Exchange(2, lambda s: tgt_buf.at[me_b], lambda s: tgt_buf.at[s], tgt_send, tgt_recv)
    out = Exchange(2, lambda s: outbox.at[s], lambda s: inbox.at[s], out_send, out_recv)
    sum_b = Exchange(2, lambda s: gb_buf.at[me_b], lambda s: gb_buf.at[s], gb_send, gb_recv)
    sum_a = Exchange(3, lambda s: ga_buf.at[me_a], lambda s: ga_buf.at[s], ga_send, ga_recv)

    cosine = cosine_ref[...]
    azimuth = azimuth_ref[...]
    radius = radius_ref[...]
    area = area_ref[...]
    sine_part = jnp.sqrt(jnp.maximum(1.0 - cosine * cosine, 0.0))
    pos0 = radius * (sine_part * jnp.cos(azimuth))
    pos1 = radius * (sine_part * jnp.sin(azimuth))
    pos2 = radius * cosine
    weight = (-0.75 / math.pi) * (area * spacing) / (2.0 * radius)
    nothing = jnp.zeros((3, WIDTH), f32)
    geo = jnp.concatenate([pos0, pos1, pos2, radius * radius, weight, nothing], axis=0)
    parts = [right_ref[m] for m in range(3)] + [geo]
    own_rest = jnp.concatenate([part[:, 128:WIDTH] for part in parts], axis=1)
    for m in range(4):
        src_buf[me_a, 8 * m : 8 * m + 8, :] = parts[m][:, :128]
    src_buf[me_a, 32:40, :] = own_rest
    tgt_buf[me_b, 0:4, :] = geo[0:4, :128]
    tgt_buf[me_b, 4:5, :] = jnp.concatenate([geo[a : a + 1, 128:WIDTH] for a in range(4)], axis=1)

    pl.semaphore_wait(barrier, sum(count - 1 for _, _, count in lines[:3]))
    for k in NEAREST[:3]:
        src_z.copy(lax.rem(me_z + k, 8), me_z).start()
    tgt.start()
    for k in NEAREST[3:]:
        src_z.copy(lax.rem(me_z + k, 8), me_z).start()

    def put_sources(tile, place, parts):
        lanes = slice(128 * place, 128 * place + 128)
        geo = parts[3]
        scaled = [split(parts[c] * geo[4:5, :], 2) for c in range(3)]
        along = sum(geo[c : c + 1, :] * (scaled[c][0] + scaled[c][1]) for c in range(3))
        pieces = [scaled[c][p] for p in range(2) for c in range(3)] + split(along, 3)
        pieces.append(jnp.zeros((8, 128), f32))
        feats[tile, :, lanes] = jnp.concatenate(pieces, axis=0).astype(bf16)
        at = pl.ds(pl.multiple_of(tile * DEPTH + 128 * place, 128), 128)
        for a in range(4):
            columns[a, at, :] = jnp.transpose(jnp.broadcast_to(geo[a : a + 1, :], (128, 128)))

    def put_tile(tile, quads):
        for place, parts in enumerate(quads):
            put_sources(tile, place, parts)
    def main_sources(tile, slots):
        put_tile(tile, [[src_buf[slot, 8 * m : 8 * m + 8, :] for m in range(4)] for slot in slots])

    def rest_sources():
        quads = [
            [
                jnp.concatenate(
                    [src_buf[4 * place + d, 32:40, 32 * m : 32 * m + 32] for d in range(4)], axis=1
                )
                for m in range(4)
            ]
            for place in range(4)
        ]
        put_tile(4, quads)

    for tile in range(TARGET_TILES):
        sums[tile] = jnp.zeros((3, FEATS, COLS), f32)

    def line_sources(tile, offsets):
        for k in offsets:
            slot = lax.rem(me_z + k, 8)
            src_z.copy(slot, slot).wait_recv()
        own = [me_z] if tile == 0 else []
        main_sources(
            tile, [core * 8 + slot for slot in own + [lax.rem(me_z + k, 8) for k in offsets]]
        )

    line_sources(0, NEAREST[:3])
    def main_rows(tile):
        rows[tile] = jnp.concatenate([tgt_buf[2 * tile], tgt_buf[2 * tile + 1]], axis=1)

    def all_rows():
        for tile in range(8):
            main_rows(tile)
        for tile in range(2):
            for a in range(4):
                rows[8 + tile, a : a + 1, :] = jnp.concatenate(
                    [tgt_buf[8 * tile + d, 4:5, 32 * a : 32 * a + 32] for d in range(8)], axis=1
                )

    tgt.wait()
    all_rows()

    def pair_parts(target_tile, source_tile, tile_ref):
        target = [rows[target_tile, a : a + 1, :] for a in range(3)]
        reach = rows[target_tile, 3:4, :] + spacing

        def one(c):
            at = pl.ds(pl.multiple_of(source_tile * DEPTH + c * CHUNK, CHUNK), CHUNK)

            def column(a):
                value = columns[a, at, :]
                return jnp.concatenate([value] * (COLS // 128), axis=1)

            r = [target[a] - column(a) for a in range(3)]
            dist = (r[0] * r[0] + spacing) + r[1] * r[1] + r[2] * r[2]
            inv = lax.rsqrt(dist)
            inv2 = inv * inv
            strength = (((reach - column(3)) - dist) * inv) * (inv2 * inv2)
            for a in range(3):
                value = strength * r[a]
                high = value.astype(bf16)
                tile_ref[a, 0, c * CHUNK : (c + 1) * CHUNK, :] = high
                tile_ref[a, 1, c * CHUNK : (c + 1) * CHUNK, :] = (value - high.astype(f32)).astype(bf16)

        return [functools.partial(one, c) for c in range(DEPTH // CHUNK)]

    def sum_parts(target_tile, source_tile, tile_ref):
        def one(a):
            left = feats[source_tile]
            sums[target_tile, a] += jnp.dot(
                left, tile_ref[a, 0], preferred_element_type=f32
            ) + jnp.dot(left, tile_ref[a, 1], preferred_element_type=f32)

        return [functools.partial(one, a) for a in range(3)]

    def mixed(firsts, seconds):
        order = [((i + 0.5) / len(firsts), 0, f) for i, f in enumerate(firsts)]
        order += [((i + 0.3) / len(seconds), 1, f) for i, f in enumerate(seconds)]
        for _, _, f in sorted(order, key=lambda item: item[:2]):
            f()

    def images(tile):
        found = []
        for a in range(3):
            total = sums[tile, a]
            image = -(total[48:56] + total[56:64] + total[64:72])
            for c in range(3):
                image = image + rows[tile, c : c + 1, :] * (
                    total[8 * c : 8 * c + 8] + total[24 + 8 * c : 32 + 8 * c]
                )
            found.append(image)
        return found

    pairs = TARGET_TILES // 2
    turns = pairs * SOURCE_TILES

    def place_of(turn):
        source = lax.div(turn, pairs)
        pair = lax.rem(turn, pairs)
        near_first = jnp.where(pair == pairs - 1, pairs - 1, lax.rem(me_y + pair, LINE))
        near_last = jnp.where(pair == 0, pairs - 1, lax.rem(me_y + pair, LINE))
        return source, 2 * jnp.where(source == SOURCE_TILES - 1, near_last, near_first)

    first_source, first_target = place_of(0)
    for f in pair_parts(first_target, first_source, tile_a):
        f()

    def advance(turn, carry):
        source, target = place_of(turn)
        later_source, later_target = place_of(jnp.minimum(turn + 1, turns - 1))

        @pl.when(turn == pairs - 1)
        def _():
            line_sources(1, NEAREST[3:])
            src_core.start()

        @pl.when(turn == 2 * pairs - 1)
        def _():
            src_core.wait()

            def far(tile, carry):
                main_sources(tile, [(1 - core) * 8 + (tile - 2) * 4 + k for k in range(4)])
                return carry

            lax.fori_loop(2, 4, far, 0)
            rest_sources()

        @pl.when(turn < turns)
        def _():
            mixed(pair_parts(target + 1, source, tile_b), sum_parts(target, source, tile_a))

        @pl.when(turn < turns + 1)
        def _():
            mixed(
                pair_parts(later_target, later_source, tile_a),
                sum_parts(target + 1, source, tile_b),
            )

        last = source == SOURCE_TILES - 1

        @pl.when(jnp.logical_and(last, target == 8))
        def _():
            for tile in range(2):
                found = images(8 + tile)
                for d in range(8):
                    lanes = slice(32 * d, 32 * d + 32)
                    outbox[8 * tile + d, 24:32, :] = jnp.concatenate(
                        [found[a][:, lanes] for a in range(3)] + [jnp.zeros((8, 32), f32)], axis=1
                    )

        @pl.when(jnp.logical_and(last, target < 8))
        def _():
            for tile in range(2):
                found = images(target + tile)
                for half in range(2):
                    for a in range(3):
                        outbox[2 * (target + tile) + half, 8 * a : 8 * a + 8, :] = found[a][
                            :, 128 * half : 128 * half + 128
                        ]

        @pl.when(jnp.logical_and(last, target < 8))
        def _():
            def push(x, carry):
                slot = 2 * target + lax.rem(me_x + x, LINE)

                @pl.when(slot != me_b)
                def _():
                    out.copy(slot, me_b).start()

                return carry

            lax.fori_loop(0, LINE, push, 0)

        return carry

    lax.fori_loop(0, turns, advance, 0)

    inbox[me_b] = outbox[me_b]
    for exchange in (tgt, src_z, src_core, out):
        exchange.finish()
    out.wait()
    image = inbox[0]
    for slot in range(1, GROUP):
        image = image + inbox[slot]

    lane = lax.broadcasted_iota(jnp.int32, (8, 128), 1)
    own = [src_buf[me_a, 8 * m : 8 * m + 8, :] for m in range(3)]
    own.append(jnp.where(lane < 96, src_buf[me_a, 32:40, :], 0.0))
    right = jnp.concatenate(own, axis=1)
    pushed = jnp.concatenate([image[8 * m : 8 * m + 8, :] for m in range(4)], axis=1)
    both = jnp.concatenate([right, pushed], axis=0)
    gram = exact_dot(both, both, ((1,), (1,)))
    gram = jnp.concatenate([gram[0:8], gram[8:16]], axis=1)
    gram = jnp.concatenate([gram[2 * m : 2 * m + 2] for m in range(4)], axis=1)
    for total, buf in ((sum_b, gb_buf), (sum_a, ga_buf)):
        buf[total.mine] = gram
        total.start()
        total.wait()
        gram = buf[0]
        for slot in range(1, GROUP):
            gram = gram + buf[slot]
    gram = jnp.concatenate([gram[:, 32 * m : 32 * m + 32] for m in range(4)], axis=0)

    row8 = lax.broadcasted_iota(jnp.int32, (8, 8), 0)
    lane8 = lax.broadcasted_iota(jnp.int32, (8, 8), 1)
    unit = jnp.where(row8 == lane8, 1.0, 0.0)
    first = eliminate(jnp.concatenate([gram[:, 0:8], unit, gram[:, 8:16]], axis=1))
    inverse = first[:, 8:16]
    moved = exact_dot(first[:, 16:24], inverse, ((1,), (1,)))
    image_gram = exact_dot(
        exact_dot(inverse, gram[:, 24:32], ((1,), (0,))), inverse, ((1,), (1,))
    )
    remainder_gram = image_gram - exact_dot(moved, moved, ((0,), (0,)))
    back = exact_dot(moved, inverse, ((0,), (0,)))
    second = eliminate(jnp.concatenate([remainder_gram, inverse, -back], axis=1))
    stacked = jnp.concatenate([pushed, right], axis=0)
    result = exact_dot(second[:, 8:24], stacked, ((1,), (0,)))
    for c in range(3):
        next_ref[c, :, 0:128] = result[:, 128 * c : 128 * c + 128]
        next_ref[c, :, 128:WIDTH] = result[:, 384 + 32 * c : 416 + 32 * c]
    coef_ref[0:8, :] = jnp.where(lane8 >= row8, first[:, 0:8], 0.0)
    coef_ref[8:16, :] = moved + 0.5 * unit
    coef_ref[16:24, :] = jnp.where(lane8 >= row8, second[:, 0:8], 0.0)

    for exchange in (sum_b, sum_a):
        exchange.finish()


def shards(right_sides, cosine, azimuth, radius, panel_area):
    width = cosine.shape[0]
    total = width * lax.axis_size("row") * lax.axis_size("col")
    spacing = 4.0 * math.pi / total
    next_block, coefficients = pl.pallas_call(
        functools.partial(kernel, spacing),
        out_shape=(
            jax.ShapeDtypeStruct((3, 8, width), f32),
            jax.ShapeDtypeStruct((24, 8), f32),
        ),
        in_specs=[pl.BlockSpec(memory_space=pltpu.VMEM)] * 5,
        out_specs=(pl.BlockSpec(memory_space=pltpu.VMEM), pl.BlockSpec(memory_space=pltpu.VMEM)),
        scratch_shapes=[
            pltpu.VMEM((GROUP, 40, 128), f32),
            pltpu.VMEM((GROUP, 8, 128), f32),
            pltpu.VMEM((4, SOURCES, 128), f32),
            pltpu.VMEM((SOURCE_TILES, FEATS, DEPTH), bf16),
            pltpu.VMEM((TARGET_TILES, 8, COLS), f32),
            pltpu.VMEM((3, 2, DEPTH, COLS), bf16),
            pltpu.VMEM((3, 2, DEPTH, COLS), bf16),
            pltpu.VMEM((TARGET_TILES, 3, FEATS, COLS), f32),
            pltpu.VMEM((GROUP, 32, 128), f32),
            pltpu.VMEM((GROUP, 32, 128), f32),
            pltpu.VMEM((GROUP, 2, 128), f32),
            pltpu.VMEM((GROUP, 2, 128), f32),
        ]
        + [pltpu.SemaphoreType.DMA((GROUP,))] * 12,
        compiler_params=pltpu.CompilerParams(
            collective_id=0, has_side_effects=True, vmem_limit_bytes=40 << 20
        ),
        name="arnoldi_step",
    )(jnp.transpose(right_sides, (1, 0, 2)), *[v.reshape(1, width) for v in (cosine, azimuth, radius, panel_area)])
    return jnp.transpose(next_block, (1, 0, 2)), coefficients


def solution(mesh):
    placed = (
        P(None, None, ("row", "col")),
        P(("row", "col")),
        P(("row", "col")),
        P(("row", "col")),
        P(("row", "col")),
    )
    return jax.shard_map(
        shards,
        mesh=mesh,
        in_specs=placed,
        out_specs=(P(None, None, ("row", "col")), P()),
        check_vma=False,
    )
```

```python
import functools
import math

import jax
import jax.numpy as jnp
from jax import lax
from jax.experimental import pallas as pl
from jax.experimental.pallas import tpu as pltpu
from jax.sharding import PartitionSpec as P

f32 = jnp.float32
bf16 = jnp.bfloat16
MESH = pl.DeviceIdType.MESH
NEAREST = (1, 7, 2, 6, 3, 5, 4)
LINE = 4
GROUP = 16
WIDTH = 160
SOURCES = GROUP * WIDTH
TARGETS = GROUP * WIDTH
COLS = 256
DEPTH = 512
CHUNK = 32
FEATS = 80
TARGET_TILES = TARGETS // COLS
SOURCE_TILES = SOURCES // DEPTH


def exact_dot(left, right, dims):
    return lax.dot_general(
        left, right, (dims, ((), ())), precision=lax.Precision.HIGHEST, preferred_element_type=f32
    )


def split(value, pieces):
    parts = []
    for _ in range(pieces):
        part = value.astype(bf16).astype(f32)
        parts.append(part)
        value = value - part
    return parts


def eliminate(matrix):
    row = lax.broadcasted_iota(jnp.int32, matrix.shape, 0)
    for k in range(8):
        scale = 1.0 / jnp.sqrt(matrix[k : k + 1, k : k + 1])
        pivot = matrix[k : k + 1, :] * scale
        column = matrix[:, k : k + 1] * scale
        matrix = jnp.where(row == k, pivot, jnp.where(row > k, matrix - column * pivot, matrix))
    return matrix


def kernel(
    spacing,
    right_ref,
    cosine_ref,
    azimuth_ref,
    radius_ref,
    area_ref,
    next_ref,
    coef_ref,
    src_buf,
    tgt_buf,
    columns,
    feats,
    rows,
    tile_a,
    tile_b,
    sums,
    outbox,
    inbox,
    gb_buf,
    ga_buf,
    sz_send,
    sz_recv,
    sc_send,
    sc_recv,
    tgt_send,
    tgt_recv,
    out_send,
    out_recv,
    gb_send,
    gb_recv,
    ga_send,
    ga_recv,
):
    me_row = lax.axis_index("row")
    me_x = lax.axis_index("col")
    core = lax.rem(me_row, 2)
    me_y = lax.rem(lax.div(me_row, 2), LINE)
    me_z = lax.div(me_row, 8)
    me_a = core * 8 + me_z
    me_b = me_y * LINE + me_x

    def peer_z(slot):
        return (slot * 8 + me_y * 2 + core, me_x)

    def peer_core(slot):
        return (me_z * 8 + me_y * 2 + slot, me_x)

    def peer_a(slot):
        return (lax.rem(slot, 8) * 8 + me_y * 2 + lax.div(slot, 8), me_x)

    def peer_b(slot):
        return (me_z * 8 + lax.div(slot, LINE) * 2 + core, lax.rem(slot, LINE))

    lines = ((peer_z, me_z, 8), (peer_core, core, 2), (peer_b, me_b, GROUP), (peer_a, me_a, GROUP))
    barrier = pltpu.get_barrier_semaphore()
    for peer, mine, count in lines[:3]:

        def greet(k, carry, peer=peer, mine=mine, count=count):
            pl.semaphore_signal(
                barrier, inc=1, device_id=peer(lax.rem(mine + k, count)), device_id_type=MESH
            )
            return carry

        lax.fori_loop(1, count, greet, 0)

    class Exchange:
        def __init__(self, line, src_of, dst_of, send, recv):
            self.peer, self.mine, self.count = lines[line]
            self.src_of, self.dst_of, self.send, self.recv = src_of, dst_of, send, recv

        def copy(self, slot, landing):
            return pltpu.make_async_remote_copy(
                src_ref=self.src_of(slot),
                dst_ref=self.dst_of(landing),
                send_sem=self.send.at[slot],
                recv_sem=self.recv.at[landing],
                device_id=self.peer(slot),
                device_id_type=MESH,
            )

        def each(self, act):
            def one(k, carry):
                act(lax.rem(self.mine + k, self.count))
                return carry

            lax.fori_loop(1, self.count, one, 0)

        def start(self):
            far_first = sorted(range(1, self.count), key=lambda k: (-min(k, self.count - k), k))
            for k in far_first:
                self.copy(lax.rem(self.mine + k, self.count), self.mine).start()

        def wait(self):
            self.each(lambda slot: self.copy(slot, slot).wait_recv())

        def finish(self):
            self.each(lambda slot: self.copy(slot, slot).wait_send())

    def group(buf, slot, count):
        return buf.at[pl.ds(slot * count, count)]

    src_z = Exchange(
        0, lambda s: src_buf.at[me_a], lambda s: src_buf.at[core * 8 + s], sz_send, sz_recv
    )
    src_core = Exchange(
        1, lambda s: group(src_buf, core, 8), lambda s: group(src_buf, s, 8), sc_send, sc_recv
    )
    tgt = Exchange(2, lambda s: tgt_buf.at[me_b], lambda s: tgt_buf.at[s], tgt_send, tgt_recv)
    out = Exchange(2, lambda s: outbox.at[s], lambda s: inbox.at[s], out_send, out_recv)
    sum_b = Exchange(2, lambda s: gb_buf.at[me_b], lambda s: gb_buf.at[s], gb_send, gb_recv)
    sum_a = Exchange(3, lambda s: ga_buf.at[me_a], lambda s: ga_buf.at[s], ga_send, ga_recv)

    cosine = cosine_ref[...]
    azimuth = azimuth_ref[...]
    radius = radius_ref[...]
    area = area_ref[...]
    sine_part = jnp.sqrt(jnp.maximum(1.0 - cosine * cosine, 0.0))
    pos0 = radius * (sine_part * jnp.cos(azimuth))
    pos1 = radius * (sine_part * jnp.sin(azimuth))
    pos2 = radius * cosine
    weight = (-0.75 / math.pi) * (area * spacing) / (2.0 * radius)
    nothing = jnp.zeros((3, WIDTH), f32)
    geo = jnp.concatenate([pos0, pos1, pos2, radius * radius, weight, nothing], axis=0)
    parts = [right_ref[m] for m in range(3)] + [geo]
    own_rest = jnp.concatenate([part[:, 128:WIDTH] for part in parts], axis=1)
    for m in range(4):
        src_buf[me_a, 8 * m : 8 * m + 8, :] = parts[m][:, :128]
    src_buf[me_a, 32:40, :] = own_rest
    tgt_buf[me_b, 0:4, :] = geo[0:4, :128]
    tgt_buf[me_b, 4:5, :] = jnp.concatenate([geo[a : a + 1, 128:WIDTH] for a in range(4)], axis=1)

    pl.semaphore_wait(barrier, sum(count - 1 for _, _, count in lines[:3]))
    def same_y(act):
        for k in range(1, LINE):
            act(me_y * LINE + lax.rem(me_x + k, LINE))

    def other_y(act):
        def one(k, carry):
            y = lax.rem(me_y + 1 + lax.div(k, LINE), LINE)
            act(y * LINE + lax.rem(me_x + k, LINE))
            return carry

        lax.fori_loop(0, GROUP - LINE, one, 0)

    def tgt_start(slot):
        tgt.copy(slot, me_b).start()

    def tgt_wait(slot):
        tgt.copy(slot, slot).wait_recv()

    same_y(tgt_start)
    for k in NEAREST[:3]:
        src_z.copy(lax.rem(me_z + 8 - k, 8), me_z).start()
    other_y(tgt_start)
    for k in NEAREST[3:]:
        src_z.copy(lax.rem(me_z + 8 - k, 8), me_z).start()

    def put_sources(tile, place, parts):
        lanes = slice(128 * place, 128 * place + 128)
        geo = parts[3]
        scaled = [split(parts[c] * geo[4:5, :], 2) for c in range(3)]
        along = sum(geo[c : c + 1, :] * (scaled[c][0] + scaled[c][1]) for c in range(3))
        pieces = [scaled[c][p] for p in range(2) for c in range(3)] + split(along, 3)
        pieces.append(jnp.zeros((8, 128), f32))
        feats[tile, :, lanes] = jnp.concatenate(pieces, axis=0).astype(bf16)
        at = pl.ds(pl.multiple_of(tile * DEPTH + 128 * place, 128), 128)
        for a in range(4):
            columns[a, at, :] = jnp.transpose(jnp.broadcast_to(geo[a : a + 1, :], (128, 128)))

    def put_tile(tile, quads):
        for place, parts in enumerate(quads):
            put_sources(tile, place, parts)
    def main_sources(tile, slots):
        put_tile(tile, [[src_buf[slot, 8 * m : 8 * m + 8, :] for m in range(4)] for slot in slots])

    def rest_sources():
        quads = [
            [
                jnp.concatenate(
                    [src_buf[4 * place + d, 32:40, 32 * m : 32 * m + 32] for d in range(4)], axis=1
                )
                for m in range(4)
            ]
            for place in range(4)
        ]
        put_tile(4, quads)

    for tile in range(TARGET_TILES):
        sums[tile] = jnp.zeros((3, FEATS, COLS), f32)

    def line_sources(tile, offsets):
        for k in offsets:
            slot = lax.rem(me_z + k, 8)
            src_z.copy(slot, slot).wait_recv()
        own = [me_z] if tile == 0 else []
        main_sources(
            tile, [core * 8 + slot for slot in own + [lax.rem(me_z + k, 8) for k in offsets]]
        )

    line_sources(0, NEAREST[:3])
    def main_rows(tile):
        rows[tile] = jnp.concatenate([tgt_buf[2 * tile], tgt_buf[2 * tile + 1]], axis=1)

    def all_rows():
        for tile in range(8):
            main_rows(tile)
        for tile in range(2):
            for a in range(4):
                rows[8 + tile, a : a + 1, :] = jnp.concatenate(
                    [tgt_buf[8 * tile + d, 4:5, 32 * a : 32 * a + 32] for d in range(8)], axis=1
                )

    same_y(tgt_wait)
    for tile in range(2):
        main_rows(2 * me_y + tile)

    def pair_parts(target_tile, source_tile, tile_ref):
        target = [rows[target_tile, a : a + 1, :] for a in range(3)]
        reach = rows[target_tile, 3:4, :] + spacing

        def one(c):
            at = pl.ds(pl.multiple_of(source_tile * DEPTH + c * CHUNK, CHUNK), CHUNK)

            def column(a):
                value = columns[a, at, :]
                return jnp.concatenate([value] * (COLS // 128), axis=1)

            r = [target[a] - column(a) for a in range(3)]
            dist = (r[0] * r[0] + spacing) + r[1] * r[1] + r[2] * r[2]
            inv = lax.rsqrt(dist)
            inv2 = inv * inv
            strength = (((reach - column(3)) - dist) * inv) * (inv2 * inv2)
            for a in range(3):
                value = strength * r[a]
                high = value.astype(bf16)
                tile_ref[a, 0, c * CHUNK : (c + 1) * CHUNK, :] = high
                tile_ref[a, 1, c * CHUNK : (c + 1) * CHUNK, :] = (value - high.astype(f32)).astype(bf16)

        return [functools.partial(one, c) for c in range(DEPTH // CHUNK)]

    def sum_parts(target_tile, source_tile, tile_ref):
        def one(a):
            left = feats[source_tile]
            sums[target_tile, a] += jnp.dot(
                left, tile_ref[a, 0], preferred_element_type=f32
            ) + jnp.dot(left, tile_ref[a, 1], preferred_element_type=f32)

        return [functools.partial(one, a) for a in range(3)]

    def mixed(firsts, seconds):
        order = [((i + 0.5) / len(firsts), 0, f) for i, f in enumerate(firsts)]
        order += [((i + 0.3) / len(seconds), 1, f) for i, f in enumerate(seconds)]
        for _, _, f in sorted(order, key=lambda item: item[:2]):
            f()

    def images(tile):
        found = []
        for a in range(3):
            total = sums[tile, a]
            image = -(total[48:56] + total[56:64] + total[64:72])
            for c in range(3):
                image = image + rows[tile, c : c + 1, :] * (
                    total[8 * c : 8 * c + 8] + total[24 + 8 * c : 32 + 8 * c]
                )
            found.append(image)
        return found

    pairs = TARGET_TILES // 2
    turns = pairs * SOURCE_TILES

    def place_of(turn):
        source = lax.div(turn, pairs)
        pair = lax.rem(turn, pairs)
        near_first = jnp.where(pair == pairs - 1, pairs - 1, lax.rem(me_y + pair, LINE))
        near_last = jnp.where(pair == 0, pairs - 1, lax.rem(me_y + pair, LINE))
        return source, 2 * jnp.where(source == SOURCE_TILES - 1, near_last, near_first)

    first_source, first_target = place_of(0)
    for f in pair_parts(first_target, first_source, tile_a):
        f()

    def advance(turn, carry):
        source, target = place_of(turn)
        later_source, later_target = place_of(jnp.minimum(turn + 1, turns - 1))

        @pl.when(lax.rem(turn, pairs) == pairs - 1)
        def _():
            @pl.when(turn == pairs - 1)
            def _():
                line_sources(1, NEAREST[3:])
                src_core.start()

            @pl.when(turn == 2 * pairs - 1)
            def _():
                src_core.wait()

                def far(tile, carry):
                    main_sources(tile, [(1 - core) * 8 + (tile - 2) * 4 + k for k in range(4)])
                    return carry

                lax.fori_loop(2, 4, far, 0)
                rest_sources()

        @pl.when(turn < turns)
        def _():
            mixed(pair_parts(target + 1, source, tile_b), sum_parts(target, source, tile_a))

        @pl.when(turn == 0)
        def _():
            other_y(tgt_wait)
            all_rows()

        @pl.when(turn < turns + 1)
        def _():
            mixed(
                pair_parts(later_target, later_source, tile_a),
                sum_parts(target + 1, source, tile_b),
            )

        last = source == SOURCE_TILES - 1

        @pl.when(last)
        def _():
            @pl.when(target == 8)
            def _():
                for tile in range(2):
                    found = images(8 + tile)
                    for d in range(8):
                        lanes = slice(32 * d, 32 * d + 32)
                        outbox[8 * tile + d, 24:32, :] = jnp.concatenate(
                            [found[a][:, lanes] for a in range(3)] + [jnp.zeros((8, 32), f32)], axis=1
                        )

            @pl.when(target < 8)
            def _():
                for tile in range(2):
                    found = images(target + tile)
                    for half in range(2):
                        for a in range(3):
                            outbox[2 * (target + tile) + half, 8 * a : 8 * a + 8, :] = found[a][
                                :, 128 * half : 128 * half + 128
                            ]

            @pl.when(target < 8)
            def _():
                def push(x, carry):
                    slot = 2 * target + lax.rem(me_x + x, LINE)

                    @pl.when(slot != me_b)
                    def _():
                        out.copy(slot, me_b).start()

                    return carry

                lax.fori_loop(0, LINE, push, 0)

        return carry

    lax.fori_loop(0, turns, advance, 0)

    inbox[me_b] = outbox[me_b]
    for exchange in (tgt, src_z, src_core, out):
        exchange.finish()
    out.wait()
    image = inbox[0]
    for slot in range(1, GROUP):
        image = image + inbox[slot]

    lane = lax.broadcasted_iota(jnp.int32, (8, 128), 1)
    own = [src_buf[me_a, 8 * m : 8 * m + 8, :] for m in range(3)]
    own.append(jnp.where(lane < 96, src_buf[me_a, 32:40, :], 0.0))
    right = jnp.concatenate(own, axis=1)
    pushed = jnp.concatenate([image[8 * m : 8 * m + 8, :] for m in range(4)], axis=1)
    both = jnp.concatenate([right, pushed], axis=0)
    gram = exact_dot(both, both, ((1,), (1,)))
    gram = jnp.concatenate([gram[0:8], gram[8:16]], axis=1)
    gram = jnp.concatenate([gram[2 * m : 2 * m + 2] for m in range(4)], axis=1)
    for total, buf in ((sum_b, gb_buf), (sum_a, ga_buf)):
        buf[total.mine] = gram
        total.start()
        total.wait()
        gram = buf[0]
        for slot in range(1, GROUP):
            gram = gram + buf[slot]
    gram = jnp.concatenate([gram[:, 32 * m : 32 * m + 32] for m in range(4)], axis=0)

    row8 = lax.broadcasted_iota(jnp.int32, (8, 8), 0)
    lane8 = lax.broadcasted_iota(jnp.int32, (8, 8), 1)
    unit = jnp.where(row8 == lane8, 1.0, 0.0)
    first = eliminate(jnp.concatenate([gram[:, 0:8], unit, gram[:, 8:16]], axis=1))
    inverse = first[:, 8:16]
    moved = exact_dot(first[:, 16:24], inverse, ((1,), (1,)))
    image_gram = exact_dot(
        exact_dot(inverse, gram[:, 24:32], ((1,), (0,))), inverse, ((1,), (1,))
    )
    remainder_gram = image_gram - exact_dot(moved, moved, ((0,), (0,)))
    back = exact_dot(moved, inverse, ((0,), (0,)))
    second = eliminate(jnp.concatenate([remainder_gram, inverse, -back], axis=1))
    stacked = jnp.concatenate([pushed, right], axis=0)
    result = exact_dot(second[:, 8:24], stacked, ((1,), (0,)))
    for c in range(3):
        next_ref[c, :, 0:128] = result[:, 128 * c : 128 * c + 128]
        next_ref[c, :, 128:WIDTH] = result[:, 384 + 32 * c : 416 + 32 * c]
    coef_ref[0:8, :] = jnp.where(lane8 >= row8, first[:, 0:8], 0.0)
    coef_ref[8:16, :] = moved + 0.5 * unit
    coef_ref[16:24, :] = jnp.where(lane8 >= row8, second[:, 0:8], 0.0)

    for exchange in (sum_b, sum_a):
        exchange.finish()


def shards(right_sides, cosine, azimuth, radius, panel_area):
    width = cosine.shape[0]
    total = width * lax.axis_size("row") * lax.axis_size("col")
    spacing = 4.0 * math.pi / total
    next_block, coefficients = pl.pallas_call(
        functools.partial(kernel, spacing),
        out_shape=(
            jax.ShapeDtypeStruct((3, 8, width), f32),
            jax.ShapeDtypeStruct((24, 8), f32),
        ),
        in_specs=[pl.BlockSpec(memory_space=pltpu.VMEM)] * 5,
        out_specs=(pl.BlockSpec(memory_space=pltpu.VMEM), pl.BlockSpec(memory_space=pltpu.VMEM)),
        scratch_shapes=[
            pltpu.VMEM((GROUP, 40, 128), f32),
            pltpu.VMEM((GROUP, 8, 128), f32),
            pltpu.VMEM((4, SOURCES, 128), f32),
            pltpu.VMEM((SOURCE_TILES, FEATS, DEPTH), bf16),
            pltpu.VMEM((TARGET_TILES, 8, COLS), f32),
            pltpu.VMEM((3, 2, DEPTH, COLS), bf16),
            pltpu.VMEM((3, 2, DEPTH, COLS), bf16),
            pltpu.VMEM((TARGET_TILES, 3, FEATS, COLS), f32),
            pltpu.VMEM((GROUP, 32, 128), f32),
            pltpu.VMEM((GROUP, 32, 128), f32),
            pltpu.VMEM((GROUP, 2, 128), f32),
            pltpu.VMEM((GROUP, 2, 128), f32),
        ]
        + [pltpu.SemaphoreType.DMA((GROUP,))] * 12,
        compiler_params=pltpu.CompilerParams(
            collective_id=0, has_side_effects=True, vmem_limit_bytes=40 << 20
        ),
        name="arnoldi_step",
    )(jnp.transpose(right_sides, (1, 0, 2)), *[v.reshape(1, width) for v in (cosine, azimuth, radius, panel_area)])
    return jnp.transpose(next_block, (1, 0, 2)), coefficients


def solution(mesh):
    placed = (
        P(None, None, ("row", "col")),
        P(("row", "col")),
        P(("row", "col")),
        P(("row", "col")),
        P(("row", "col")),
    )
    return jax.shard_map(
        shards,
        mesh=mesh,
        in_specs=placed,
        out_specs=(P(None, None, ("row", "col")), P()),
        check_vma=False,
    )
```

```python
import functools
import math

import jax
import jax.numpy as jnp
from jax import lax
from jax.experimental import pallas as pl
from jax.experimental.pallas import tpu as pltpu
from jax.sharding import PartitionSpec as P

f32 = jnp.float32
bf16 = jnp.bfloat16
MESH = pl.DeviceIdType.MESH
NEAREST = (1, 7, 2, 6, 3, 5, 4)
LINE = 4
GROUP = 16
WIDTH = 160
SOURCES = GROUP * WIDTH
TARGETS = GROUP * WIDTH
COLS = 256
DEPTH = 512
CHUNK = 32
FEATS = 80
TARGET_TILES = TARGETS // COLS
SOURCE_TILES = SOURCES // DEPTH


def exact_dot(left, right, dims):
    return lax.dot_general(
        left, right, (dims, ((), ())), precision=lax.Precision.HIGHEST, preferred_element_type=f32
    )


def split(value, pieces):
    parts = []
    for _ in range(pieces):
        part = value.astype(bf16).astype(f32)
        parts.append(part)
        value = value - part
    return parts


def eliminate(matrix):
    row = lax.broadcasted_iota(jnp.int32, matrix.shape, 0)
    for k in range(8):
        scale = 1.0 / jnp.sqrt(matrix[k : k + 1, k : k + 1])
        pivot = matrix[k : k + 1, :] * scale
        column = matrix[:, k : k + 1] * scale
        matrix = jnp.where(row == k, pivot, jnp.where(row > k, matrix - column * pivot, matrix))
    return matrix


def kernel(
    spacing,
    right_ref,
    cosine_ref,
    azimuth_ref,
    radius_ref,
    area_ref,
    next_ref,
    coef_ref,
    src_buf,
    tgt_buf,
    columns,
    feats,
    rows,
    tile_a,
    tile_b,
    sums,
    outbox,
    inbox,
    gb_buf,
    ga_buf,
    sz_send,
    sz_recv,
    sc_send,
    sc_recv,
    tgt_send,
    tgt_recv,
    out_send,
    out_recv,
    gb_send,
    gb_recv,
    ga_send,
    ga_recv,
):
    me_row = lax.axis_index("row")
    me_x = lax.axis_index("col")
    core = lax.rem(me_row, 2)
    me_y = lax.rem(lax.div(me_row, 2), LINE)
    me_z = lax.div(me_row, 8)
    me_a = core * 8 + me_z
    me_b = me_y * LINE + me_x

    def peer_z(slot):
        return (slot * 8 + me_y * 2 + core, me_x)

    def peer_core(slot):
        return (me_z * 8 + me_y * 2 + slot, me_x)

    def peer_a(slot):
        return (lax.rem(slot, 8) * 8 + me_y * 2 + lax.div(slot, 8), me_x)

    def peer_b(slot):
        return (me_z * 8 + lax.div(slot, LINE) * 2 + core, lax.rem(slot, LINE))

    lines = ((peer_z, me_z, 8), (peer_core, core, 2), (peer_b, me_b, GROUP), (peer_a, me_a, GROUP))
    barrier = pltpu.get_barrier_semaphore()
    for peer, mine, count in lines[:3]:

        def greet(k, carry, peer=peer, mine=mine, count=count):
            pl.semaphore_signal(
                barrier, inc=1, device_id=peer(lax.rem(mine + k, count)), device_id_type=MESH
            )
            return carry

        lax.fori_loop(1, count, greet, 0)

    class Exchange:
        def __init__(self, line, src_of, dst_of, send, recv):
            self.peer, self.mine, self.count = lines[line]
            self.src_of, self.dst_of, self.send, self.recv = src_of, dst_of, send, recv

        def copy(self, slot, landing):
            return pltpu.make_async_remote_copy(
                src_ref=self.src_of(slot),
                dst_ref=self.dst_of(landing),
                send_sem=self.send.at[slot],
                recv_sem=self.recv.at[landing],
                device_id=self.peer(slot),
                device_id_type=MESH,
            )

        def each(self, act):
            def one(k, carry):
                act(lax.rem(self.mine + k, self.count))
                return carry

            lax.fori_loop(1, self.count, one, 0)

        def start(self):
            far_first = sorted(range(1, self.count), key=lambda k: (-min(k, self.count - k), k))
            for k in far_first:
                self.copy(lax.rem(self.mine + k, self.count), self.mine).start()

        def wait(self):
            self.each(lambda slot: self.copy(slot, slot).wait_recv())

        def finish(self):
            self.each(lambda slot: self.copy(slot, slot).wait_send())

    def group(buf, slot, count):
        return buf.at[pl.ds(slot * count, count)]

    src_z = Exchange(
        0, lambda s: src_buf.at[me_a], lambda s: src_buf.at[core * 8 + s], sz_send, sz_recv
    )
    src_core = Exchange(
        1, lambda s: group(src_buf, core, 8), lambda s: group(src_buf, s, 8), sc_send, sc_recv
    )
    tgt = Exchange(2, lambda s: tgt_buf.at[me_b], lambda s: tgt_buf.at[s], tgt_send, tgt_recv)
    out = Exchange(2, lambda s: outbox.at[s], lambda s: inbox.at[s], out_send, out_recv)
    sum_b = Exchange(2, lambda s: gb_buf.at[me_b], lambda s: gb_buf.at[s], gb_send, gb_recv)
    sum_a = Exchange(3, lambda s: ga_buf.at[me_a], lambda s: ga_buf.at[s], ga_send, ga_recv)

    cosine = cosine_ref[...]
    azimuth = azimuth_ref[...]
    radius = radius_ref[...]
    area = area_ref[...]
    sine_part = jnp.sqrt(jnp.maximum(1.0 - cosine * cosine, 0.0))
    pos0 = radius * (sine_part * jnp.cos(azimuth))
    pos1 = radius * (sine_part * jnp.sin(azimuth))
    pos2 = radius * cosine
    weight = (-0.75 / math.pi) * (area * spacing) / (2.0 * radius)
    nothing = jnp.zeros((3, WIDTH), f32)
    geo = jnp.concatenate([pos0, pos1, pos2, radius * radius, weight, nothing], axis=0)
    parts = [right_ref[m] for m in range(3)] + [geo]
    own_rest = jnp.concatenate([part[:, 128:WIDTH] for part in parts], axis=1)
    for m in range(4):
        src_buf[me_a, 8 * m : 8 * m + 8, :] = parts[m][:, :128]
    src_buf[me_a, 32:40, :] = own_rest
    tgt_buf[me_b, 0:4, :] = geo[0:4, :128]
    tgt_buf[me_b, 4:5, :] = jnp.concatenate([geo[a : a + 1, 128:WIDTH] for a in range(4)], axis=1)

    pl.semaphore_wait(barrier, sum(count - 1 for _, _, count in lines[:3]))
    def same_y(act):
        for k in range(1, LINE):
            act(me_y * LINE + lax.rem(me_x + k, LINE))

    def other_y(act):
        def one(k, carry):
            y = lax.rem(me_y + 1 + lax.div(k, LINE), LINE)
            act(y * LINE + lax.rem(me_x + k, LINE))
            return carry

        lax.fori_loop(0, GROUP - LINE, one, 0)

    def tgt_start(slot):
        tgt.copy(slot, me_b).start()

    def tgt_wait(slot):
        tgt.copy(slot, slot).wait_recv()

    same_y(tgt_start)
    for k in NEAREST[:3]:
        src_z.copy(lax.rem(me_z + 8 - k, 8), me_z).start()
    other_y(tgt_start)
    for k in NEAREST[3:]:
        src_z.copy(lax.rem(me_z + 8 - k, 8), me_z).start()

    def put_sources(tile, place, parts):
        lanes = slice(128 * place, 128 * place + 128)
        geo = parts[3]
        scaled = [split(parts[c] * geo[4:5, :], 2) for c in range(3)]
        along = sum(geo[c : c + 1, :] * (scaled[c][0] + scaled[c][1]) for c in range(3))
        pieces = [scaled[c][p] for p in range(2) for c in range(3)] + split(along, 3)
        pieces.append(jnp.zeros((8, 128), f32))
        feats[tile, :, lanes] = jnp.concatenate(pieces, axis=0).astype(bf16)
        at = pl.ds(pl.multiple_of(tile * DEPTH + 128 * place, 128), 128)
        for a in range(4):
            columns[a, at, :] = jnp.transpose(jnp.broadcast_to(geo[a : a + 1, :], (128, 128)))

    def put_tile(tile, quads):
        for place, parts in enumerate(quads):
            put_sources(tile, place, parts)
    def main_sources(tile, slots):
        put_tile(tile, [[src_buf[slot, 8 * m : 8 * m + 8, :] for m in range(4)] for slot in slots])

    def rest_sources():
        quads = [
            [
                jnp.concatenate(
                    [src_buf[4 * place + d, 32:40, 32 * m : 32 * m + 32] for d in range(4)], axis=1
                )
                for m in range(4)
            ]
            for place in range(4)
        ]
        put_tile(4, quads)

    for tile in range(TARGET_TILES):
        sums[tile] = jnp.zeros((3, FEATS, COLS), f32)

    def line_sources(tile, offsets):
        for k in offsets:
            slot = lax.rem(me_z + k, 8)
            src_z.copy(slot, slot).wait_recv()
        own = [me_z] if tile == 0 else []
        main_sources(
            tile, [core * 8 + slot for slot in own + [lax.rem(me_z + k, 8) for k in offsets]]
        )

    line_sources(0, NEAREST[:3])
    def main_rows(tile):
        rows[tile] = jnp.concatenate([tgt_buf[2 * tile], tgt_buf[2 * tile + 1]], axis=1)

    def all_rows():
        for tile in range(8):
            main_rows(tile)
        for tile in range(2):
            for a in range(4):
                rows[8 + tile, a : a + 1, :] = jnp.concatenate(
                    [tgt_buf[8 * tile + d, 4:5, 32 * a : 32 * a + 32] for d in range(8)], axis=1
                )

    same_y(tgt_wait)
    for tile in range(2):
        main_rows(2 * me_y + tile)

    def pair_parts(target_tile, source_tile, tile_ref):
        target = [rows[target_tile, a : a + 1, :] for a in range(3)]
        reach = rows[target_tile, 3:4, :] + spacing

        def one(c):
            at = pl.ds(pl.multiple_of(source_tile * DEPTH + c * CHUNK, CHUNK), CHUNK)

            def column(a):
                value = columns[a, at, :]
                return jnp.concatenate([value] * (COLS // 128), axis=1)

            r = [target[a] - column(a) for a in range(3)]
            dist = (r[0] * r[0] + spacing) + r[1] * r[1] + r[2] * r[2]
            inv = lax.rsqrt(dist)
            inv2 = inv * inv
            strength = (((reach - column(3)) - dist) * inv) * (inv2 * inv2)
            for a in range(3):
                value = strength * r[a]
                high = value.astype(bf16)
                tile_ref[a, 0, c * CHUNK : (c + 1) * CHUNK, :] = high
                tile_ref[a, 1, c * CHUNK : (c + 1) * CHUNK, :] = (value - high.astype(f32)).astype(bf16)

        return [functools.partial(one, c) for c in range(DEPTH // CHUNK)]

    def sum_parts(target_tile, source_tile, tile_ref):
        def one(a):
            left = feats[source_tile]
            sums[target_tile, a] += jnp.dot(
                left, tile_ref[a, 0], preferred_element_type=f32
            ) + jnp.dot(left, tile_ref[a, 1], preferred_element_type=f32)

        return [functools.partial(one, a) for a in range(3)]

    def mixed(firsts, seconds):
        order = [((i + 0.5) / len(firsts), 0, f) for i, f in enumerate(firsts)]
        order += [((i + 0.3) / len(seconds), 1, f) for i, f in enumerate(seconds)]
        for _, _, f in sorted(order, key=lambda item: item[:2]):
            f()

    def images(tile):
        found = []
        for a in range(3):
            total = sums[tile, a]
            image = -(total[48:56] + total[56:64] + total[64:72])
            for c in range(3):
                image = image + rows[tile, c : c + 1, :] * (
                    total[8 * c : 8 * c + 8] + total[24 + 8 * c : 32 + 8 * c]
                )
            found.append(image)
        return found

    pairs = TARGET_TILES // 2
    turns = pairs * SOURCE_TILES

    def place_of(turn):
        source = lax.div(turn, pairs)
        pair = lax.rem(turn, pairs)
        near_first = jnp.where(pair == pairs - 1, pairs - 1, lax.rem(me_y + pair, LINE))
        near_last = jnp.where(pair == 0, pairs - 1, lax.rem(me_y + pair, LINE))
        return source, 2 * jnp.where(source == SOURCE_TILES - 1, near_last, near_first)

    first_source, first_target = place_of(0)
    for f in pair_parts(first_target, first_source, tile_a):
        f()

    def advance(turn, carry):
        source, target = place_of(turn)
        later_source, later_target = place_of(jnp.minimum(turn + 1, turns - 1))

        @pl.when(lax.rem(turn, pairs) == pairs - 1)
        def _():
            @pl.when(turn == pairs - 1)
            def _():
                line_sources(1, NEAREST[3:])
                src_core.start()

            @pl.when(turn == 2 * pairs - 1)
            def _():
                src_core.wait()

                def far(tile, carry):
                    main_sources(tile, [(1 - core) * 8 + (tile - 2) * 4 + k for k in range(4)])
                    return carry

                lax.fori_loop(2, 4, far, 0)
                rest_sources()

        @pl.when(turn < turns)
        def _():
            mixed(pair_parts(target + 1, source, tile_b), sum_parts(target, source, tile_a))

        @pl.when(turn == 0)
        def _():
            other_y(tgt_wait)
            all_rows()

        @pl.when(turn < turns + 1)
        def _():
            mixed(
                pair_parts(later_target, later_source, tile_a),
                sum_parts(target + 1, source, tile_b),
            )

        last = source == SOURCE_TILES - 1

        @pl.when(last)
        def _():
            @pl.when(target == 8)
            def _():
                for tile in range(2):
                    found = images(8 + tile)
                    for d in range(8):
                        lanes = slice(32 * d, 32 * d + 32)
                        outbox[8 * tile + d, 24:32, :] = jnp.concatenate(
                            [found[a][:, lanes] for a in range(3)] + [jnp.zeros((8, 32), f32)], axis=1
                        )

            @pl.when(target < 8)
            def _():
                for tile in range(2):
                    found = images(target + tile)
                    for half in range(2):
                        for a in range(3):
                            outbox[2 * (target + tile) + half, 8 * a : 8 * a + 8, :] = found[a][
                                :, 128 * half : 128 * half + 128
                            ]

            @pl.when(target < 8)
            def _():
                def push(x, carry):
                    slot = 2 * target + lax.rem(me_x + x, LINE)

                    @pl.when(slot != me_b)
                    def _():
                        out.copy(slot, me_b).start()

                    return carry

                lax.fori_loop(0, LINE, push, 0)

        return carry

    lax.fori_loop(0, turns, advance, 0)

    inbox[me_b] = outbox[me_b]
    for exchange in (tgt, src_z, src_core, out):
        exchange.finish()
    out.wait()
    image = inbox[0]
    for slot in range(1, GROUP):
        image = image + inbox[slot]

    lane = lax.broadcasted_iota(jnp.int32, (8, 128), 1)
    own = [src_buf[me_a, 8 * m : 8 * m + 8, :] for m in range(3)]
    own.append(jnp.where(lane < 96, src_buf[me_a, 32:40, :], 0.0))
    right = jnp.concatenate(own, axis=1)
    pushed = jnp.concatenate([image[8 * m : 8 * m + 8, :] for m in range(4)], axis=1)
    both = jnp.concatenate([right, pushed], axis=0)
    gram = exact_dot(both, both, ((1,), (1,)))
    gram = jnp.concatenate([gram[0:8], gram[8:16]], axis=1)
    gram = jnp.concatenate([gram[2 * m : 2 * m + 2] for m in range(4)], axis=1)
    for total, buf in ((sum_b, gb_buf), (sum_a, ga_buf)):
        buf[total.mine] = gram
        total.start()
        total.finish()
        total.wait()
        gram = buf[0]
        for slot in range(1, GROUP):
            gram = gram + buf[slot]
    gram = jnp.concatenate([gram[:, 32 * m : 32 * m + 32] for m in range(4)], axis=0)

    row8 = lax.broadcasted_iota(jnp.int32, (8, 8), 0)
    lane8 = lax.broadcasted_iota(jnp.int32, (8, 8), 1)
    unit = jnp.where(row8 == lane8, 1.0, 0.0)
    first = eliminate(jnp.concatenate([gram[:, 0:8], unit, gram[:, 8:16]], axis=1))
    inverse = first[:, 8:16]
    moved = exact_dot(first[:, 16:24], inverse, ((1,), (1,)))
    image_gram = exact_dot(
        exact_dot(inverse, gram[:, 24:32], ((1,), (0,))), inverse, ((1,), (1,))
    )
    remainder_gram = image_gram - exact_dot(moved, moved, ((0,), (0,)))
    back = exact_dot(moved, inverse, ((0,), (0,)))
    second = eliminate(jnp.concatenate([remainder_gram, inverse, -back], axis=1))
    stacked = jnp.concatenate([pushed, right], axis=0)
    result = exact_dot(second[:, 8:24], stacked, ((1,), (0,)))
    for c in range(3):
        next_ref[c, :, 0:128] = result[:, 128 * c : 128 * c + 128]
        next_ref[c, :, 128:WIDTH] = result[:, 384 + 32 * c : 416 + 32 * c]
    coef_ref[0:8, :] = jnp.where(lane8 >= row8, first[:, 0:8], 0.0)
    coef_ref[8:16, :] = moved + 0.5 * unit
    coef_ref[16:24, :] = jnp.where(lane8 >= row8, second[:, 0:8], 0.0)


def shards(right_sides, cosine, azimuth, radius, panel_area):
    width = cosine.shape[0]
    total = width * lax.axis_size("row") * lax.axis_size("col")
    spacing = 4.0 * math.pi / total
    next_block, coefficients = pl.pallas_call(
        functools.partial(kernel, spacing),
        out_shape=(
            jax.ShapeDtypeStruct((3, 8, width), f32),
            jax.ShapeDtypeStruct((24, 8), f32),
        ),
        in_specs=[pl.BlockSpec(memory_space=pltpu.VMEM)] * 5,
        out_specs=(pl.BlockSpec(memory_space=pltpu.VMEM), pl.BlockSpec(memory_space=pltpu.VMEM)),
        scratch_shapes=[
            pltpu.VMEM((GROUP, 40, 128), f32),
            pltpu.VMEM((GROUP, 8, 128), f32),
            pltpu.VMEM((4, SOURCES, 128), f32),
            pltpu.VMEM((SOURCE_TILES, FEATS, DEPTH), bf16),
            pltpu.VMEM((TARGET_TILES, 8, COLS), f32),
            pltpu.VMEM((3, 2, DEPTH, COLS), bf16),
            pltpu.VMEM((3, 2, DEPTH, COLS), bf16),
            pltpu.VMEM((TARGET_TILES, 3, FEATS, COLS), f32),
            pltpu.VMEM((GROUP, 32, 128), f32),
            pltpu.VMEM((GROUP, 32, 128), f32),
            pltpu.VMEM((GROUP, 2, 128), f32),
            pltpu.VMEM((GROUP, 2, 128), f32),
        ]
        + [pltpu.SemaphoreType.DMA((GROUP,))] * 12,
        compiler_params=pltpu.CompilerParams(
            collective_id=0, has_side_effects=True, vmem_limit_bytes=40 << 20
        ),
        name="arnoldi_step",
    )(jnp.transpose(right_sides, (1, 0, 2)), *[v.reshape(1, width) for v in (cosine, azimuth, radius, panel_area)])
    return jnp.transpose(next_block, (1, 0, 2)), coefficients


def solution(mesh):
    placed = (
        P(None, None, ("row", "col")),
        P(("row", "col")),
        P(("row", "col")),
        P(("row", "col")),
        P(("row", "col")),
    )
    return jax.shard_map(
        shards,
        mesh=mesh,
        in_specs=placed,
        out_specs=(P(None, None, ("row", "col")), P()),
        check_vma=False,
    )
```
